512 devices in a mesh: wide: 32 (over z, core), narrow: 16 (over y, x).
Axes of the slice: x: 4, y: 4, z: 16, core: 2. Of those that a mesh axis runs over, the one named last changes fastest.
Arguments:
- vectors: bfloat16 [64, 2097152], P(None, ('wide', 'narrow'))
- anchors: float32 [2097152], P(('wide', 'narrow')), may hold values from 0.5 to 4
- pins: int32 [8, 2621440], P(None, ('wide', 'narrow')), may hold values from -1 to 6143, as said below
- halo_rows: int32 [2, 524288], P(None, ('wide', 'narrow')), may hold values from 0 to 4095, as said below
Outputs:
- embedding: float32 [64, 2097152], P(None, ('wide', 'narrow'))
- r_factor: float32 [64, 64], replicated
The draws below stay inside these ranges and needn't reach their ends.
Inputs may be any that keep to these rules, and one draw needn't show every extreme that they name: Each net lists 2 to 8 valid pins first, then -1; the first net of every partition has 8 pins and the second 2; pins index the extended list of the net's own partition, and the first net of every partition names its last entry. `halo_rows`: each partition's list for each direction holds 1024 distinct rows of that partition.
All inputs are finite; a program needn't handle non-finite values.
Results may differ from the reference program's by a relative error of at most 0.00096.
Values may be sent and summed in bfloat16 or wider, within the bound.
No kernel may reach another device: no remote copies, remote signals or barrier semaphores. Data moves between devices by JAX's collectives and lax.ppermute only.
A program may use at most 64 MiB of HBM per device.

```python
import math
import jax
import jax.numpy as jnp
from jax import lax

CELLS_DEV = 4096
K = 64
PINS = 8
BOUND = 1024
NETS_DEV = 5120
CELLS = 2097152
NETS = 2621440


def chain_rows(fresh):
    carried = fresh[0]
    rows = [carried]
    keep = math.sqrt(1.0 - 0.49)
    for index in range(1, K):
        carried = 0.7 * carried + keep * fresh[index]
        rows.append(carried)
    return jnp.stack(rows, axis=0)


def draw_vectors(key, part):
    key = jax.random.fold_in(key, 11)
    first, second, third = jax.random.split(key, 3)
    position = jnp.arange(CELLS, dtype=jnp.float32) / CELLS
    column_scale = jnp.exp(jax.random.uniform(second, (K,), minval=0.0, maxval=math.log(10.0)))
    row_scale = jnp.exp(jax.random.uniform(third, (CELLS,), minval=0.0, maxval=math.log(10.0)))
    fresh = jnp.clip(jax.random.normal(first, (K, CELLS)), -5.0, 5.0)
    base = chain_rows(fresh)
    rising = jnp.sqrt(1.0 + 2.0 * position)
    values = 0.05 * base * column_scale[:, None] * (row_scale * rising)[None, :]
    return values.astype(jnp.bfloat16)


def draw_pins(key, part):
    key = jax.random.fold_in(key, 23)
    first, second, third, fourth = jax.random.split(key, 4)
    extent = CELLS_DEV + 2 * BOUND
    size = jax.random.randint(first, (NETS,), 2, PINS + 1)
    net_place = jnp.arange(NETS) % NETS_DEV
    size = jnp.where(net_place == 0, PINS, jnp.where(net_place == 1, 2, size))
    local = jax.random.randint(second, (PINS, NETS), 0, CELLS_DEV)
    remote = jax.random.randint(third, (PINS, NETS), CELLS_DEV, extent)
    pick = jax.random.randint(fourth, (PINS, NETS), 0, 8)
    slot = jnp.arange(PINS)[:, None]
    chosen = jnp.where((pick == 0) & (slot > 0), remote, local)
    chosen = jnp.where((slot == PINS - 1) & (net_place[None, :] == 0), extent - 1, chosen)
    return jnp.where(slot < size[None, :], chosen, -1).astype(jnp.int32)


def draw_halo_rows(key, part):
    key = jax.random.fold_in(key, 37)
    parts = CELLS // CELLS_DEV
    keys = jax.random.split(key, 2 * parts)
    chosen = jax.vmap(lambda single: jax.random.permutation(single, CELLS_DEV)[:BOUND])(keys)
    return chosen.reshape(2, parts * BOUND).astype(jnp.int32)


def steps_of(stream_key, shape, cuts, least, high):
    level = 1.0
    for dim, blocks in cuts:
        steps = jax.random.uniform(jax.random.fold_in(jax.random.fold_in(stream_key, 6), dim), (blocks,), jnp.float32, least / len(cuts), high / len(cuts))
        level = level * jnp.repeat(jnp.exp(steps), shape[dim] // blocks).reshape((-1,) + (1,) * (len(shape) - 1 - dim))
    return level


def setup_inputs(seed: int = 0) -> dict:
    seeds = jax.random.split(jax.random.key(seed), 5)
    vectors = draw_vectors(jax.random.fold_in(seeds[4], 71), 0)
    anchors = jnp.clip(jnp.exp(math.log(4.0) - 2.0794415 * jax.random.uniform(seeds[1], (CELLS,), jnp.float32) ** steps_of(seeds[1], (CELLS,), ((0, 512),), -0.2, 0.2)), 0.5, 4.0)
    pins = draw_pins(jax.random.fold_in(seeds[4], 71), 0)
    halo_rows = draw_halo_rows(jax.random.fold_in(seeds[4], 71), 0)
    return {"vectors": vectors, "anchors": anchors, "pins": pins, "halo_rows": halo_rows}


def apply_part(extended, pins_part, anchor_part, own):
    total = extended.shape[0]
    valid = pins_part >= 0
    safe = jnp.where(valid, pins_part, total).astype(jnp.int32)
    padded = jnp.concatenate([extended.astype(jnp.float32), jnp.zeros((1, K), jnp.float32)], axis=0)
    sums = lax.optimization_barrier(jnp.sum(padded[safe], axis=1))
    size = lax.optimization_barrier(jnp.sum(valid.astype(jnp.float32), axis=1))
    weight = 1.0 / (size - 1.0)
    scaled = (sums * weight[:, None]).astype(jnp.bfloat16)
    scaled = lax.optimization_barrier(scaled).astype(jnp.float32)
    local = valid & (pins_part < CELLS_DEV)
    target = jnp.where(local, pins_part, CELLS_DEV).astype(jnp.int32).reshape(-1)
    spread = jnp.broadcast_to(scaled[:, None, :], (NETS_DEV, PINS, K)).reshape(-1, K)
    contrib = jax.ops.segment_sum(spread, target, num_segments=CELLS_DEV + 1)[:CELLS_DEV]
    degree_terms = jnp.broadcast_to((weight * size)[:, None], (NETS_DEV, PINS)).reshape(-1)
    degree = jax.ops.segment_sum(degree_terms, target, num_segments=CELLS_DEV + 1)[:CELLS_DEV]
    return (degree + anchor_part)[:, None] * own.astype(jnp.float32) - contrib

def reference(vectors, anchors, pins, halo_rows):
    parts = CELLS // CELLS_DEV
    blocks = vectors.reshape(K, parts, CELLS_DEV).transpose(1, 2, 0)
    lists = halo_rows.reshape(2, parts, BOUND).astype(jnp.int32)
    up_rows = jnp.take_along_axis(blocks, lists[0][:, :, None], axis=1)
    down_rows = jnp.take_along_axis(blocks, lists[1][:, :, None], axis=1)
    from_prev = jnp.roll(up_rows, 1, axis=0)
    from_next = jnp.roll(down_rows, -1, axis=0)
    extended = jnp.concatenate([blocks, from_prev, from_next], axis=1)
    pin_parts = pins.reshape(PINS, parts, NETS_DEV).transpose(1, 2, 0)
    anchor_parts = anchors.reshape(parts, CELLS_DEV)

    def one_part(items):
        return apply_part(items[0], items[1], items[2], items[3])
    images = lax.map(one_part, (extended, pin_parts, anchor_parts, blocks))
    image = images.reshape(CELLS, K)
    gram = jnp.dot(image.T.astype(jnp.float32), image.astype(jnp.float32), precision=lax.Precision.HIGHEST, preferred_element_type=jnp.float32)
    factor = jnp.linalg.cholesky(gram).T
    inverse = lax.linalg.triangular_solve(factor, jnp.eye(K, dtype=jnp.float32), left_side=True, lower=False)
    scale = jnp.sqrt(jnp.float32(CELLS))
    embedding = scale * jnp.dot(image.astype(jnp.float32), inverse.astype(jnp.float32), precision=lax.Precision.HIGHEST, preferred_element_type=jnp.float32)
    return (embedding.T, factor / scale)
```

```python
import functools

import jax
import jax.numpy as jnp
from jax import lax
from jax.experimental import pallas as pl
from jax.experimental.pallas import tpu as pltpu
from jax.sharding import PartitionSpec as P

BOTH = ("wide", "narrow")
HIGHEST = lax.Precision.HIGHEST
BLOCK = 512
CHUNK = 1024
VMEM_LIMIT = 60 << 20


def shifted(value, steps):
    count = lax.axis_size(BOTH)
    pairs = [(source, (source + steps) % count) for source in range(count)]
    return lax.ppermute(value, BOTH, pairs)


def image_kernel(
    pins_ref, vectors_ref, prev_ref, next_ref, anchors_ref,
    image_ref, gram_ref,
    extended, contrib, inc_even, inc_odd, pin_tile, count_tile, t_even, t_odd, sums,
):
    width, cells = vectors_ref.shape
    bound = prev_ref.shape[1]
    total = cells + 2 * bound
    slots, nets = pins_ref.shape
    incs = (inc_even, inc_odd)
    scaled = (t_even, t_odd)
    blocks = nets // BLOCK

    extended[:, :cells] = vectors_ref[...]
    extended[:, cells : cells + bound] = prev_ref[...]
    extended[:, cells + bound :] = next_ref[...]
    contrib[...] = jnp.zeros_like(contrib)

    def prepare(block):
        pins = pins_ref[:, block * BLOCK : (block + 1) * BLOCK]
        count = jnp.zeros((slots, BLOCK), jnp.int32)
        for slot in range(slots):
            count = count + (pins == pins[slot : slot + 1, :]).astype(jnp.int32)
        for slot in range(slots):
            row = pins[slot : slot + 1, :]
            pin_tile[slot] = jnp.broadcast_to(row, (16, BLOCK)).astype(jnp.int16)
            times = count[slot : slot + 1, :].astype(jnp.float32)
            count_tile[slot] = jnp.broadcast_to(times, (16, BLOCK)).astype(jnp.bfloat16)
        sums[...] = jnp.zeros_like(sums)

    def build(chunk):
        start = (chunk * CHUNK).astype(jnp.int16)
        local = [pin_tile[slot] - start for slot in range(slots)]
        lane = lax.broadcasted_iota(jnp.int32, (16, BLOCK), 0).astype(jnp.int16)
        rows = []
        for row in range(CHUNK // 16):
            place = lane + jnp.int16(16 * row)
            value = jnp.zeros((16, BLOCK), jnp.bfloat16)
            for slot in range(slots):
                value = jnp.where(local[slot] == place, count_tile[slot], value)
            rows.append(value)
        return jnp.concatenate(rows, axis=0)

    def finish(block):
        pins = pins_ref[:, block * BLOCK : (block + 1) * BLOCK]
        size = jnp.sum((pins >= 0).astype(jnp.float32), axis=0, keepdims=True)
        weight = 1.0 / (size - 1.0)
        target = scaled[block % 2]
        target[:width, :] = (sums[...] * weight).astype(jnp.bfloat16)
        degree = weight * size
        first = degree.astype(jnp.bfloat16).astype(jnp.float32)
        second = (degree - first).astype(jnp.bfloat16).astype(jnp.float32)
        third = degree - first - second
        row = lax.broadcasted_iota(jnp.int32, (16, BLOCK), 0)
        parts = jnp.where(row == 0, first, jnp.where(row == 1, second, jnp.where(row == 2, third, 0.0)))
        target[width:, :] = parts.astype(jnp.bfloat16)

    def step(block, spread, chunk):
        base = pl.multiple_of(chunk * CHUNK, CHUNK)
        if spread:
            added = lax.dot_general(
                scaled[1 - block % 2][...],
                incs[1 - block % 2][pl.ds(base, CHUNK), :],
                (((1,), (1,)), ((), ())),
                preferred_element_type=jnp.float32,
            )
        if block < blocks:
            tile = build(chunk)
            incs[block % 2][pl.ds(base, CHUNK), :] = tile
            sums[...] += jnp.dot(
                extended[:, pl.ds(base, CHUNK)], tile, preferred_element_type=jnp.float32
            )
        if spread:
            contrib[:, pl.ds(base, CHUNK)] += added

    for block in range(blocks + 1):
        if block < blocks:
            prepare(block)

        def near(chunk, carry):
            step(block, block > 0, chunk)
            return carry

        def far(chunk, carry):
            step(block, False, chunk)
            return carry

        lax.fori_loop(0, cells // CHUNK, near, 0)
        if block < blocks:
            lax.fori_loop(cells // CHUNK, total // CHUNK, far, 0)
            finish(block)

    degree = contrib[width : width + 1, :] + contrib[width + 1 : width + 2, :] + contrib[width + 2 : width + 3, :]
    image = (degree + anchors_ref[...]) * vectors_ref[...].astype(jnp.float32) - contrib[:width, :]
    image_ref[...] = image
    gram_ref[...] = lax.dot_general(
        image, image, (((1,), (1,)), ((), ())), precision=HIGHEST, preferred_element_type=jnp.float32
    )


def image_and_gram(pins, vectors, from_prev, from_next, anchors):
    width, cells = vectors.shape
    total = cells + 2 * from_prev.shape[1]
    slots = pins.shape[0]
    whole = pl.BlockSpec(memory_space=pltpu.VMEM)
    return pl.pallas_call(
        image_kernel,
        out_shape=(
            jax.ShapeDtypeStruct((width, cells), jnp.float32),
            jax.ShapeDtypeStruct((width, width), jnp.float32),
        ),
        in_specs=[whole] * 5,
        out_specs=(whole, whole),
        scratch_shapes=[
            pltpu.VMEM((width, total), jnp.bfloat16),
            pltpu.VMEM((width + 16, cells), jnp.float32),
            pltpu.VMEM((total, BLOCK), jnp.bfloat16),
            pltpu.VMEM((total, BLOCK), jnp.bfloat16),
            pltpu.VMEM((slots, 16, BLOCK), jnp.int16),
            pltpu.VMEM((slots, 16, BLOCK), jnp.bfloat16),
            pltpu.VMEM((width + 16, BLOCK), jnp.bfloat16),
            pltpu.VMEM((width + 16, BLOCK), jnp.bfloat16),
            pltpu.VMEM((width, BLOCK), jnp.float32),
        ],
        compiler_params=pltpu.CompilerParams(vmem_limit_bytes=VMEM_LIMIT),
    )(pins, vectors, from_prev, from_next, anchors[None, :])


def factor_kernel(scale, gram_ref, image_ref, embedding_ref, factor_ref):
    width = gram_ref.shape[0]
    rows = lax.broadcasted_iota(jnp.int32, (width, 2 * width), 0)
    columns = lax.broadcasted_iota(jnp.int32, (width, 2 * width), 1)
    unit = (columns == rows + width).astype(jnp.float32)
    work = jnp.concatenate([gram_ref[...], jnp.zeros((width, width), jnp.float32)], axis=1) + unit
    pivots = []
    for index in range(width):
        base = index // 8 * 8
        part = work[base:]
        row = work[index : index + 1]
        pivot = work[index : index + 1, index : index + 1]
        pivots.append(pivot)
        column = jnp.where(rows[base:] > index, part[:, index : index + 1], 0.0)
        part = part - column * (row * (1.0 / pivot))
        work = jnp.concatenate([work[:base], part], axis=0) if base else part
    work = work / jnp.sqrt(jnp.concatenate(pivots, axis=0))
    upper = columns[:, :width] >= rows[:, :width]
    factor_ref[...] = jnp.where(upper, work[:, :width], 0.0) / scale
    embedding_ref[...] = jnp.dot(
        work[:, width:] * scale, image_ref[...], precision=HIGHEST, preferred_element_type=jnp.float32
    )


def factor_and_embed(gram, image, scale):
    whole = pl.BlockSpec(memory_space=pltpu.VMEM)
    return pl.pallas_call(
        functools.partial(factor_kernel, scale),
        out_shape=(
            jax.ShapeDtypeStruct(image.shape, jnp.float32),
            jax.ShapeDtypeStruct(gram.shape, jnp.float32),
        ),
        in_specs=[whole, whole],
        out_specs=(whole, whole),
        compiler_params=pltpu.CompilerParams(vmem_limit_bytes=VMEM_LIMIT),
    )(gram, image)


def body(vectors, anchors, pins, halo_rows):
    cells = vectors.shape[1]
    up = jnp.take(vectors, halo_rows[0], axis=1)
    down = jnp.take(vectors, halo_rows[1], axis=1)
    from_prev = shifted(up, 1)
    from_next = shifted(down, -1)
    image, gram = image_and_gram(pins, vectors, from_prev, from_next, anchors)
    gram = jnp.sum(lax.all_gather(gram, "narrow"), axis=0)
    gram = jnp.sum(lax.all_gather(gram, "wide"), axis=0)
    scale = float(cells * lax.axis_size(BOTH)) ** 0.5
    return factor_and_embed(gram, image, scale)


def solution(mesh):
    in_specs = (P(None, BOTH), P(BOTH), P(None, BOTH), P(None, BOTH))
    out_specs = (P(None, BOTH), P())
    return jax.shard_map(body, mesh=mesh, in_specs=in_specs, out_specs=out_specs, check_vma=False)
```

```python
import functools

import jax
import jax.numpy as jnp
from jax import lax
from jax.experimental import pallas as pl
from jax.experimental.pallas import tpu as pltpu
from jax.sharding import PartitionSpec as P

BOTH = ("wide", "narrow")
HIGHEST = lax.Precision.HIGHEST
BLOCK = 512
CHUNK = 256
FIELDS = 4
PICK = 512
SPAN = 4096
AHEAD = 2
VMEM_LIMIT = 60 << 20


def shifted(value, steps):
    count = lax.axis_size(BOTH)
    pairs = [(source, (source + steps) % count) for source in range(count)]
    return lax.ppermute(value, BOTH, pairs)


def pick_kernel(rows_ref, vectors_ref, up_ref, down_ref):
    width, cells = vectors_ref.shape
    count = rows_ref.shape[1]
    lane = lax.broadcasted_iota(jnp.int32, (16, PICK), 0).astype(jnp.int16)
    for direction, picked_ref in enumerate((up_ref, down_ref)):
        for part in range(count // PICK):
            columns = slice(part * PICK, (part + 1) * PICK)
            wanted = rows_ref[direction : direction + 1, columns]
            wanted = jnp.broadcast_to(wanted, (16, PICK)).astype(jnp.int16)

            def step(chunk, total):
                base = pl.multiple_of(chunk * SPAN, SPAN)
                local = wanted - (chunk * SPAN).astype(jnp.int16)
                tile = [
                    jnp.where(local == lane + jnp.int16(16 * row), jnp.bfloat16(1), jnp.bfloat16(0))
                    for row in range(SPAN // 16)
                ]
                return total + jnp.dot(
                    vectors_ref[:, pl.ds(base, SPAN)],
                    jnp.concatenate(tile, axis=0),
                    preferred_element_type=jnp.float32,
                )

            total = lax.fori_loop(0, cells // SPAN, step, jnp.zeros((width, PICK), jnp.float32))
            picked_ref[:, columns] = total.astype(jnp.bfloat16)


def pick(halo_rows, vectors):
    whole = pl.BlockSpec(memory_space=pltpu.VMEM)
    width, cells = vectors.shape
    count = halo_rows.shape[1]
    picked = jax.ShapeDtypeStruct((width, count), jnp.bfloat16)
    return pl.pallas_call(
        pick_kernel,
        out_shape=(picked, picked),
        in_specs=[whole, whole],
        out_specs=(whole, whole),
        cost_estimate=pl.CostEstimate(
            flops=4 * width * cells * count, bytes_accessed=2 * width * cells, transcendentals=0
        ),
        compiler_params=pltpu.CompilerParams(vmem_limit_bytes=VMEM_LIMIT),
    )(halo_rows, vectors)


def spread_pins(stride, pins, place_tile, value_tile):
    slots, block = pins.shape
    field = jnp.zeros(pins.shape, jnp.int32)
    for index in range(1, FIELDS):
        field = field + (pins >= index * stride).astype(jnp.int32)
    place = pins - field * stride
    value = jnp.where(field == 0, 1, jnp.where(field == 1, 16, jnp.where(field == 2, 256, 4096)))
    for slot in range(slots):
        place_tile[slot] = jnp.broadcast_to(place[slot : slot + 1, :], (16, block)).astype(jnp.int16)
        value_tile[slot] = jnp.broadcast_to(value[slot : slot + 1, :], (16, block)).astype(jnp.int16)


def build_words(chunk, extent, place_tile, value_tile):
    slots, sublanes, block = place_tile.shape
    lane = lax.broadcasted_iota(jnp.int32, (sublanes, block), 0).astype(jnp.int16)
    local = [place_tile[slot] - (chunk * extent).astype(jnp.int16) for slot in range(slots)]
    rows = []
    for row in range(extent // sublanes):
        here = lane + jnp.int16(sublanes * row)
        word = jnp.zeros((sublanes, block), jnp.int16)
        for slot in range(slots):
            word = word + jnp.where(local[slot] == here, value_tile[slot], jnp.int16(0))
        rows.append(word)
    return jnp.concatenate(rows, axis=0)


def words_kernel(pins_ref, words_ref, place_tile, value_tile):
    stride = words_ref.shape[0]
    spread_pins(stride, pins_ref[...], place_tile, value_tile)

    def step(chunk, carry):
        words_ref[pl.ds(pl.multiple_of(chunk * 512, 512), 512), :] = build_words(
            chunk, 512, place_tile, value_tile
        )
        return carry

    lax.fori_loop(0, stride // 512, step, 0)


def count_words(pins, total):
    slots = pins.shape[0]
    nets = 2 * BLOCK * AHEAD
    stride = total // FIELDS
    return pl.pallas_call(
        words_kernel,
        grid=(nets // BLOCK,),
        out_shape=jax.ShapeDtypeStruct((stride, nets), jnp.int16),
        in_specs=[pl.BlockSpec((slots, BLOCK), lambda step: (0, step))],
        out_specs=pl.BlockSpec((stride, BLOCK), lambda step: (0, step)),
        scratch_shapes=[pltpu.VMEM((slots, 16, BLOCK), jnp.int16)] * 2,
        cost_estimate=pl.CostEstimate(
            flops=24 * stride * nets, bytes_accessed=2 * stride * nets, transcendentals=0
        ),
        compiler_params=pltpu.CompilerParams(vmem_limit_bytes=VMEM_LIMIT),
    )(pins)


def image_kernel(
    words_ref, pins_ref, vectors_ref, prev_ref, next_ref, anchors_ref,
    image_ref, gram_ref,
    extended, contrib, inc_even, inc_odd, t_even, t_odd, sums, place_tile, value_tile,
):
    width, cells = vectors_ref.shape
    bound = prev_ref.shape[1]
    stride = words_ref.shape[0]
    incs = (inc_even, inc_odd)
    scaled = (t_even, t_odd)
    turn = pl.program_id(0)

    def finish(half):
        pins = pins_ref[:, half * BLOCK : (half + 1) * BLOCK]
        size = jnp.sum((pins >= 0).astype(jnp.float32), axis=0, keepdims=True)
        weight = 1.0 / (size - 1.0)
        target = scaled[half]
        target[:width, :] = (sums[...] * weight).astype(jnp.bfloat16)
        degree = weight * size
        first = degree.astype(jnp.bfloat16).astype(jnp.float32)
        second = (degree - first).astype(jnp.bfloat16).astype(jnp.float32)
        third = degree - first - second
        row = lax.broadcasted_iota(jnp.int32, (16, BLOCK), 0)
        parts = jnp.where(row == 0, first, jnp.where(row == 1, second, jnp.where(row == 2, third, 0.0)))
        target[width:, :] = parts.astype(jnp.bfloat16)

    def step(half, unpack, spread, owned, ahead, chunk):
        base = pl.multiple_of(chunk * CHUNK, CHUNK)
        added = []
        if spread is not None:
            for field in range(owned):
                place = pl.multiple_of(field * stride + base, CHUNK)
                added.append(
                    lax.dot_general(
                        scaled[spread][...],
                        incs[spread][pl.ds(place, CHUNK), :],
                        (((1,), (1,)), ((), ())),
                        preferred_element_type=jnp.float32,
                    )
                )
        if unpack:
            if ahead:
                words = words_ref[pl.ds(base, CHUNK), half * BLOCK : (half + 1) * BLOCK]
            else:
                words = build_words(chunk, CHUNK, place_tile, value_tile)
            fresh = jnp.zeros(sums.shape, jnp.float32)
            for field in range(FIELDS):
                place = pl.multiple_of(field * stride + base, CHUNK)
                tile = lax.shift_right_logical(words, jnp.int16(4 * field)) & jnp.int16(15)
                tile = tile.astype(jnp.bfloat16)
                if field < owned:
                    incs[half][pl.ds(place, CHUNK), :] = tile
                fresh = fresh + jnp.dot(
                    extended[:, pl.ds(place, CHUNK)], tile, preferred_element_type=jnp.float32
                )
            sums[...] += fresh
        for field, term in enumerate(added):
            place = pl.multiple_of(field * stride + base, CHUNK)
            contrib[:, pl.ds(place, CHUNK)] += term

    def sweep(half, unpack, spread, ahead):
        if unpack and not ahead:
            spread_pins(stride, pins_ref[:, half * BLOCK : (half + 1) * BLOCK], place_tile, value_tile)
        if unpack:
            sums[...] = jnp.zeros_like(sums)
        many = -(-cells // stride)
        edge = (cells - (many - 1) * stride) // CHUNK

        def low(chunk, carry):
            step(half, unpack, spread, many, ahead, chunk)
            return carry

        def high(chunk, carry):
            step(half, unpack, spread, many - 1, ahead, chunk)
            return carry

        lax.fori_loop(0, edge, low, 0)
        lax.fori_loop(edge, stride // CHUNK, high, 0)
        if unpack:
            finish(half)

    @pl.when(turn == 0)
    def _():
        extended[:, :cells] = vectors_ref[...]
        extended[:, cells : cells + bound] = prev_ref[...]
        extended[:, cells + bound :] = next_ref[...]
        contrib[...] = jnp.zeros_like(contrib)
        sweep(0, True, None, AHEAD > 0)

    @pl.when((turn > 0) & (turn < AHEAD))
    def _():
        sweep(0, True, 1, True)

    @pl.when((turn > 0) & (turn >= AHEAD))
    def _():
        sweep(0, True, 1, False)

    @pl.when(turn < AHEAD)
    def _():
        sweep(1, True, 0, True)

    @pl.when(turn >= AHEAD)
    def _():
        sweep(1, True, 0, False)

    @pl.when(turn == pl.num_programs(0) - 1)
    def _():
        sweep(1, False, 1, True)
        degree = (
            contrib[width : width + 1, :] + contrib[width + 1 : width + 2, :] + contrib[width + 2 : width + 3, :]
        )
        image = (degree + anchors_ref[...]) * vectors_ref[...].astype(jnp.float32) - contrib[:width, :]
        image_ref[...] = image
        gram = lax.dot_general(
            image, image, (((1,), (1,)), ((), ())), precision=HIGHEST, preferred_element_type=jnp.float32
        )
        fold = width // 2
        packed = jnp.concatenate([gram[:fold], gram[fold:]], axis=1)
        for copy in range(gram_ref.shape[0]):
            gram_ref[copy] = packed


def image_and_gram(words, pins, vectors, from_prev, from_next, anchors, copies):
    width, cells = vectors.shape
    slots, nets = pins.shape
    stride = words.shape[0]
    whole = pl.BlockSpec(memory_space=pltpu.VMEM)
    return pl.pallas_call(
        image_kernel,
        grid=(nets // (2 * BLOCK),),
        out_shape=(
            jax.ShapeDtypeStruct((width, cells), jnp.float32),
            jax.ShapeDtypeStruct((copies, width // 2, 2 * width), jnp.float32),
        ),
        in_specs=[
            pl.BlockSpec((stride, 2 * BLOCK), lambda step: (0, jnp.minimum(step, AHEAD - 1))),
            pl.BlockSpec((slots, 2 * BLOCK), lambda step: (0, step)),
        ]
        + [whole] * 4,
        out_specs=(whole, whole),
        scratch_shapes=[
            pltpu.VMEM((width, stride * FIELDS), jnp.bfloat16),
            pltpu.VMEM((width + 16, cells), jnp.float32),
            pltpu.VMEM((cells, BLOCK), jnp.bfloat16),
            pltpu.VMEM((cells, BLOCK), jnp.bfloat16),
            pltpu.VMEM((width + 16, BLOCK), jnp.bfloat16),
            pltpu.VMEM((width + 16, BLOCK), jnp.bfloat16),
            pltpu.VMEM((width, BLOCK), jnp.float32),
            pltpu.VMEM((slots, 16, BLOCK), jnp.int16),
            pltpu.VMEM((slots, 16, BLOCK), jnp.int16),
        ],
        compiler_params=pltpu.CompilerParams(vmem_limit_bytes=VMEM_LIMIT),
    )(words, pins, vectors, from_prev, from_next, anchors[None, :])


def summed_gram(copies):
    groups = lax.axis_size("wide")
    pairs = [[2 * chip, 2 * chip + 1] for chip in range(groups // 2)]
    columns = [[2 * chip + core for chip in range(groups // 2)] for core in range(2)]
    plane = jnp.sum(lax.all_to_all(copies, "narrow", 0, 0), axis=0)
    plane = jnp.sum(lax.all_gather(plane, "wide", axis_index_groups=pairs), axis=0)
    half = plane.shape[0] // 2
    start = lax.rem(lax.axis_index("wide"), 2) * half
    share = lax.dynamic_slice_in_dim(plane, start, half, axis=0)
    share = jnp.broadcast_to(share[None], (groups // 2,) + share.shape)
    share = jnp.sum(lax.all_to_all(share, "wide", 0, 0, axis_index_groups=columns), axis=0)
    return lax.all_gather(share, "wide", axis_index_groups=pairs, tiled=True)


def factor_kernel(scale, gram_ref, image_ref, embedding_ref, factor_ref):
    width = gram_ref.shape[1] // 2
    gram = jnp.concatenate([gram_ref[:, :width], gram_ref[:, width:]], axis=0)
    rows = lax.broadcasted_iota(jnp.int32, (width, 2 * width), 0)
    columns = lax.broadcasted_iota(jnp.int32, (width, 2 * width), 1)
    unit = (columns == rows + width).astype(jnp.float32)
    work = jnp.concatenate([gram, jnp.zeros((width, width), jnp.float32)], axis=1) + unit
    pivots = []
    for index in range(width):
        base = index // 8 * 8
        part = work[base:]
        row = work[index : index + 1]
        pivot = work[index : index + 1, index : index + 1]
        pivots.append(pivot)
        column = jnp.where(rows[base:] > index, part[:, index : index + 1], 0.0)
        part = part - column * (row * (1.0 / pivot))
        work = jnp.concatenate([work[:base], part], axis=0) if base else part
    work = work / jnp.sqrt(jnp.concatenate(pivots, axis=0))
    upper = columns[:, :width] >= rows[:, :width]
    factor_ref[...] = jnp.where(upper, work[:, :width], 0.0) / scale
    embedding_ref[...] = jnp.dot(
        work[:, width:] * scale, image_ref[...], precision=HIGHEST, preferred_element_type=jnp.float32
    )


def factor_and_embed(gram, image, scale):
    whole = pl.BlockSpec(memory_space=pltpu.VMEM)
    return pl.pallas_call(
        functools.partial(factor_kernel, scale),
        out_shape=(
            jax.ShapeDtypeStruct(image.shape, jnp.float32),
            jax.ShapeDtypeStruct((image.shape[0],) * 2, jnp.float32),
        ),
        in_specs=[whole, whole],
        out_specs=(whole, whole),
        compiler_params=pltpu.CompilerParams(vmem_limit_bytes=VMEM_LIMIT),
    )(gram, image)


def body(vectors, anchors, pins, halo_rows):
    cells = vectors.shape[1]
    total = cells + halo_rows.size
    up, down = pick(halo_rows, vectors)
    from_prev = shifted(up, 1)
    from_next = shifted(down, -1)
    words = count_words(pins, total)
    copies = lax.axis_size("narrow")
    image, gram = image_and_gram(words, pins, vectors, from_prev, from_next, anchors, copies)
    gram = summed_gram(gram)
    scale = float(cells * lax.axis_size(BOTH)) ** 0.5
    return factor_and_embed(gram, image, scale)


def solution(mesh):
    in_specs = (P(None, BOTH), P(BOTH), P(None, BOTH), P(None, BOTH))
    out_specs = (P(None, BOTH), P())
    return jax.shard_map(body, mesh=mesh, in_specs=in_specs, out_specs=out_specs, check_vma=False)
```

```python
import functools

import jax
import jax.numpy as jnp
from jax import lax
from jax.experimental import pallas as pl
from jax.experimental.pallas import tpu as pltpu
from jax.sharding import PartitionSpec as P

BOTH = ("wide", "narrow")
HIGHEST = lax.Precision.HIGHEST
BLOCK = 512
CHUNK = 256
FIELDS = 8
PICK = 512
SPAN = 4096
GROUP = 8
VMEM_LIMIT = 60 << 20


def shifted(value, steps):
    count = lax.axis_size(BOTH)
    pairs = [(source, (source + steps) % count) for source in range(count)]
    return lax.ppermute(value, BOTH, pairs)


def pick_kernel(rows_ref, vectors_ref, up_ref, down_ref):
    width, cells = vectors_ref.shape
    count = rows_ref.shape[1]
    lane = lax.broadcasted_iota(jnp.int32, (16, PICK), 0).astype(jnp.int16)
    for direction, picked_ref in enumerate((up_ref, down_ref)):
        for part in range(count // PICK):
            columns = slice(part * PICK, (part + 1) * PICK)
            wanted = rows_ref[direction : direction + 1, columns]
            wanted = jnp.broadcast_to(wanted, (16, PICK)).astype(jnp.int16)

            def step(chunk, total):
                base = pl.multiple_of(chunk * SPAN, SPAN)
                local = wanted - (chunk * SPAN).astype(jnp.int16)
                tile = [
                    jnp.where(local == lane + jnp.int16(16 * row), jnp.bfloat16(1), jnp.bfloat16(0))
                    for row in range(SPAN // 16)
                ]
                return total + jnp.dot(
                    vectors_ref[:, pl.ds(base, SPAN)],
                    jnp.concatenate(tile, axis=0),
                    preferred_element_type=jnp.float32,
                )

            total = lax.fori_loop(0, cells // SPAN, step, jnp.zeros((width, PICK), jnp.float32))
            picked_ref[:, columns] = total.astype(jnp.bfloat16)


def pick(halo_rows, vectors):
    whole = pl.BlockSpec(memory_space=pltpu.VMEM)
    width, cells = vectors.shape
    count = halo_rows.shape[1]
    picked = jax.ShapeDtypeStruct((width, count), jnp.bfloat16)
    return pl.pallas_call(
        pick_kernel,
        out_shape=(picked, picked),
        in_specs=[whole, whole],
        out_specs=(whole, whole),
        cost_estimate=pl.CostEstimate(
            flops=4 * width * cells * count, bytes_accessed=2 * width * cells, transcendentals=0
        ),
        compiler_params=pltpu.CompilerParams(vmem_limit_bytes=VMEM_LIMIT),
    )(halo_rows, vectors)


def ranks(pins):
    rows = [jnp.zeros_like(pins[:1])]
    for slot in range(1, pins.shape[0]):
        same = (pins[:slot] == pins[slot : slot + 1]).astype(jnp.int32)
        rows.append(jnp.sum(same, axis=0, keepdims=True))
    return jnp.concatenate(rows, axis=0)


def spread_pins(stride, turn, pins, place_tile, value_tile):
    slots, block = pins.shape
    field = jnp.zeros(pins.shape, jnp.int32)
    for index in range(1, FIELDS):
        field = field + (pins >= index * stride).astype(jnp.int32)
    rank = ranks(pins)
    mine = (rank >= 3 * turn) & (rank < 3 * turn + 3)
    place = jnp.where(mine, pins - field * stride, -1)
    value = lax.shift_left(jnp.ones_like(field), 2 * field)
    for slot in range(slots):
        place_tile[slot] = jnp.broadcast_to(place[slot : slot + 1, :], (16, block)).astype(jnp.int16)
        value_tile[slot] = jnp.broadcast_to(value[slot : slot + 1, :], (16, block)).astype(jnp.int16)


def build_words(chunk, extent, place_tile, value_tile):
    slots, sublanes, block = place_tile.shape
    lane = lax.broadcasted_iota(jnp.int32, (sublanes, block), 0).astype(jnp.int16)
    local = [place_tile[slot] - (chunk * extent).astype(jnp.int16) for slot in range(slots)]
    rows = []
    for row in range(extent // sublanes):
        here = lane + jnp.int16(sublanes * row)
        word = jnp.zeros((sublanes, block), jnp.int16)
        for slot in range(slots):
            word = word + jnp.where(local[slot] == here, value_tile[slot], jnp.int16(0))
        rows.append(word)
    return jnp.concatenate(rows, axis=0)


def unpack(words, field):
    return (lax.shift_right_logical(words, jnp.int16(2 * field)) & jnp.int16(3)).astype(jnp.bfloat16)


def words_kernel(pins_ref, words_ref, place_tile, value_tile):
    stride = words_ref.shape[0]
    extent = stride // 2
    spread_pins(stride, 0, pins_ref[...], place_tile, value_tile)

    def step(chunk, carry):
        words_ref[pl.ds(pl.multiple_of(chunk * extent, extent), extent), :] = build_words(
            chunk, extent, place_tile, value_tile
        )
        return carry

    lax.fori_loop(0, stride // extent, step, 0)


def count_words(pins, total):
    slots, nets = pins.shape
    stride = total // FIELDS
    return pl.pallas_call(
        words_kernel,
        grid=(nets // BLOCK,),
        out_shape=jax.ShapeDtypeStruct((stride, nets), jnp.int16),
        in_specs=[pl.BlockSpec((slots, BLOCK), lambda step: (0, step))],
        out_specs=pl.BlockSpec((stride, BLOCK), lambda step: (0, step)),
        scratch_shapes=[pltpu.VMEM((slots, 16, BLOCK), jnp.int16)] * 2,
        cost_estimate=pl.CostEstimate(
            flops=24 * stride * nets, bytes_accessed=2 * stride * nets, transcendentals=0
        ),
        compiler_params=pltpu.CompilerParams(vmem_limit_bytes=VMEM_LIMIT),
    )(pins)


def image_kernel(
    words_ref, pins_ref, vectors_ref, prev_ref, next_ref, anchors_ref,
    image_ref, gram_ref,
    extended, contrib, inc_even, inc_odd, t_even, t_odd, sums, place_tile, value_tile,
):
    width, cells = vectors_ref.shape
    bound = prev_ref.shape[1]
    stride = words_ref.shape[0]
    incs = (inc_even, inc_odd)
    scaled = (t_even, t_odd)
    turn = pl.program_id(0)

    def finish(half):
        pins = pins_ref[:, half * BLOCK : (half + 1) * BLOCK]
        size = jnp.sum((pins >= 0).astype(jnp.float32), axis=0, keepdims=True)
        weight = 1.0 / (size - 1.0)
        target = scaled[half]
        target[:width, :] = (sums[...] * weight).astype(jnp.bfloat16)
        degree = weight * size
        first = degree.astype(jnp.bfloat16).astype(jnp.float32)
        second = (degree - first).astype(jnp.bfloat16).astype(jnp.float32)
        third = degree - first - second
        row = lax.broadcasted_iota(jnp.int32, (16, BLOCK), 0)
        parts = jnp.where(row == 0, first, jnp.where(row == 1, second, jnp.where(row == 2, third, 0.0)))
        target[width:, :] = parts.astype(jnp.bfloat16)

    def step(half, gather, spread, owned, chunk):
        base = chunk * CHUNK
        added = []
        if spread is not None:
            for field in range(owned):
                place = field * stride + base
                added.append(
                    lax.dot_general(
                        scaled[spread][...],
                        incs[spread][pl.ds(place, CHUNK), :],
                        (((1,), (1,)), ((), ())),
                        preferred_element_type=jnp.float32,
                    )
                )
        if gather:
            words = words_ref[pl.ds(base, CHUNK), half * BLOCK : (half + 1) * BLOCK]
            fresh = jnp.zeros(sums.shape, jnp.float32)
            for field in range(FIELDS):
                place = field * stride + base
                tile = unpack(words, field)
                if field < owned:
                    incs[half][pl.ds(place, CHUNK), :] = tile
                fresh = fresh + jnp.dot(
                    extended[:, pl.ds(place, CHUNK)], tile, preferred_element_type=jnp.float32
                )
            sums[...] += fresh
        for field, term in enumerate(added):
            place = field * stride + base
            contrib[:, pl.ds(place, CHUNK)] += term

    def repeats(half, owned, chunk):
        base = pl.multiple_of(chunk * CHUNK, CHUNK)
        words = build_words(chunk, CHUNK, place_tile, value_tile)
        for field in range(FIELDS):
            place = pl.multiple_of(field * stride + base, CHUNK)
            tile = unpack(words, field)
            if field < owned:
                incs[half][pl.ds(place, CHUNK), :] += tile
            sums[...] += jnp.dot(extended[:, pl.ds(place, CHUNK)], tile, preferred_element_type=jnp.float32)

    many = -(-cells // stride)
    edge = (cells - (many - 1) * stride) // CHUNK

    def over_chunks(work):
        def low(chunk, carry):
            work(many, chunk)
            return carry

        def high(chunk, carry):
            work(many - 1, chunk)
            return carry

        lax.fori_loop(0, edge, low, 0)
        lax.fori_loop(edge, stride // CHUNK, high, 0)

    def sweep(half, gather, spread):
        if gather:
            sums[...] = jnp.zeros_like(sums)
        for chunk in range(stride // CHUNK):
            step(half, gather, spread, many if chunk < edge else many - 1, chunk)
        if gather:
            pins = pins_ref[:, half * BLOCK : (half + 1) * BLOCK]
            most = jnp.max(jnp.where(pins >= 0, ranks(pins), 0))

            @pl.when(most >= 3)
            def _():
                def again(later, carry):
                    spread_pins(stride, later, pins, place_tile, value_tile)
                    over_chunks(functools.partial(repeats, half))
                    return carry

                lax.fori_loop(1, 3, again, 0)

            finish(half)

    @pl.when(turn == 0)
    def _():
        extended[:, :cells] = vectors_ref[...]
        extended[:, cells : cells + bound] = prev_ref[...]
        extended[:, cells + bound :] = next_ref[...]
        contrib[...] = jnp.zeros_like(contrib)
        sweep(0, True, None)

    @pl.when(turn > 0)
    def _():
        sweep(0, True, 1)

    sweep(1, True, 0)

    @pl.when(turn == pl.num_programs(0) - 1)
    def _():
        sweep(1, False, 1)
        degree = (
            contrib[width : width + 1, :] + contrib[width + 1 : width + 2, :] + contrib[width + 2 : width + 3, :]
        )
        image = (degree + anchors_ref[...]) * vectors_ref[...].astype(jnp.float32) - contrib[:width, :]
        image_ref[...] = image
        gram = lax.dot_general(
            image, image, (((1,), (1,)), ((), ())), precision=HIGHEST, preferred_element_type=jnp.float32
        )
        fold = width // 2
        packed = jnp.concatenate([gram[:fold], gram[fold:]], axis=1)
        for copy in range(gram_ref.shape[0]):
            gram_ref[copy] = packed


def image_and_gram(words, pins, vectors, from_prev, from_next, anchors, copies):
    width, cells = vectors.shape
    slots, nets = pins.shape
    stride = words.shape[0]
    whole = pl.BlockSpec(memory_space=pltpu.VMEM)
    return pl.pallas_call(
        image_kernel,
        grid=(nets // (2 * BLOCK),),
        out_shape=(
            jax.ShapeDtypeStruct((width, cells), jnp.float32),
            jax.ShapeDtypeStruct((copies, width // 2, 2 * width), jnp.float32),
        ),
        in_specs=[
            pl.BlockSpec((stride, 2 * BLOCK), lambda step: (0, step)),
            pl.BlockSpec((slots, 2 * BLOCK), lambda step: (0, step)),
        ]
        + [whole] * 4,
        out_specs=(whole, whole),
        scratch_shapes=[
            pltpu.VMEM((width, stride * FIELDS), jnp.bfloat16),
            pltpu.VMEM((width + 16, cells), jnp.float32),
            pltpu.VMEM((cells, BLOCK), jnp.bfloat16),
            pltpu.VMEM((cells, BLOCK), jnp.bfloat16),
            pltpu.VMEM((width + 16, BLOCK), jnp.bfloat16),
            pltpu.VMEM((width + 16, BLOCK), jnp.bfloat16),
            pltpu.VMEM((width, BLOCK), jnp.float32),
            pltpu.VMEM((slots, 16, BLOCK), jnp.int16),
            pltpu.VMEM((slots, 16, BLOCK), jnp.int16),
        ],
        compiler_params=pltpu.CompilerParams(vmem_limit_bytes=VMEM_LIMIT),
    )(words, pins, vectors, from_prev, from_next, anchors[None, :])


def summed_gram(copies):
    groups = lax.axis_size("wide")
    pairs = [[2 * chip, 2 * chip + 1] for chip in range(groups // 2)]
    columns = [[2 * chip + core for chip in range(groups // 2)] for core in range(2)]
    plane = jnp.sum(lax.all_to_all(copies, "narrow", 0, 0), axis=0)
    plane = jnp.sum(lax.all_gather(plane, "wide", axis_index_groups=pairs), axis=0)
    half = plane.shape[0] // 2
    start = lax.rem(lax.axis_index("wide"), 2) * half
    share = lax.dynamic_slice_in_dim(plane, start, half, axis=0)
    share = jnp.broadcast_to(share[None], (groups // 2,) + share.shape)
    share = jnp.sum(lax.all_to_all(share, "wide", 0, 0, axis_index_groups=columns), axis=0)
    return lax.all_gather(share, "wide", axis_index_groups=pairs, tiled=True)


def factor_kernel(scale, gram_ref, image_ref, embedding_ref, factor_ref):
    width = gram_ref.shape[1] // 2
    gram = jnp.concatenate([gram_ref[:, :width], gram_ref[:, width:]], axis=0)
    rows = lax.broadcasted_iota(jnp.int32, (width, 2 * width), 0)
    columns = lax.broadcasted_iota(jnp.int32, (width, 2 * width), 1)
    unit = (columns == rows + width).astype(jnp.float32)
    work = jnp.concatenate([gram, jnp.zeros((width, width), jnp.float32)], axis=1) + unit
    pivots = []
    for index in range(0, width, GROUP):
        base = index // 8 * 8
        part = work[base:]
        below = rows[base:]
        first = index - base
        spread = [jnp.broadcast_to(part[:, index + item : index + item + 1], part.shape) for item in range(GROUP)]
        lines = [part[first + item : first + item + 1] for item in range(GROUP)]
        for item in range(GROUP):
            here = first + item
            pivot = spread[item][here : here + 1]
            pivots.append(pivot)
            inverse = 1.0 / pivot
            column = jnp.where(below > index + item, spread[item], 0.0)
            line = lines[item] * inverse
            for other in range(item + 1, GROUP):
                ratio = spread[other][here : here + 1] * inverse
                spread[other] = spread[other] - column * ratio
                lines[other] = lines[other] - column[first + other : first + other + 1] * line
            part = part - column * line
        work = jnp.concatenate([work[:base], part], axis=0) if base else part
    work = work / jnp.sqrt(jnp.concatenate(pivots, axis=0))
    upper = columns[:, :width] >= rows[:, :width]
    factor_ref[...] = jnp.where(upper, work[:, :width], 0.0) / scale
    embedding_ref[...] = jnp.dot(
        work[:, width:] * scale, image_ref[...], precision=HIGHEST, preferred_element_type=jnp.float32
    )


def factor_and_embed(gram, image, scale):
    whole = pl.BlockSpec(memory_space=pltpu.VMEM)
    return pl.pallas_call(
        functools.partial(factor_kernel, scale),
        out_shape=(
            jax.ShapeDtypeStruct(image.shape, jnp.float32),
            jax.ShapeDtypeStruct((image.shape[0],) * 2, jnp.float32),
        ),
        in_specs=[whole, whole],
        out_specs=(whole, whole),
        compiler_params=pltpu.CompilerParams(vmem_limit_bytes=VMEM_LIMIT),
    )(gram, image)


def body(vectors, anchors, pins, halo_rows):
    cells = vectors.shape[1]
    total = cells + halo_rows.size
    up, down = pick(halo_rows, vectors)
    from_prev = shifted(up, 1)
    from_next = shifted(down, -1)
    words = count_words(pins, total)
    copies = lax.axis_size("narrow")
    image, gram = image_and_gram(words, pins, vectors, from_prev, from_next, anchors, copies)
    gram = summed_gram(gram)
    scale = float(cells * lax.axis_size(BOTH)) ** 0.5
    return factor_and_embed(gram, image, scale)


def solution(mesh):
    in_specs = (P(None, BOTH), P(BOTH), P(None, BOTH), P(None, BOTH))
    out_specs = (P(None, BOTH), P())
    return jax.shard_map(body, mesh=mesh, in_specs=in_specs, out_specs=out_specs, check_vma=False)
```

```python
import functools

import jax
import jax.numpy as jnp
from jax import lax
from jax.experimental import pallas as pl
from jax.experimental.pallas import tpu as pltpu
from jax.sharding import PartitionSpec as P

BOTH = ("wide", "narrow")
HIGHEST = lax.Precision.HIGHEST
BLOCK = 512
CHUNK = 256
FIELDS = 8
PICK = 512
SPAN = 4096
GROUP = 8
VMEM_LIMIT = 60 << 20


def shifted(value, steps):
    count = lax.axis_size(BOTH)
    pairs = [(source, (source + steps) % count) for source in range(count)]
    return lax.ppermute(value, BOTH, pairs)


def pick_kernel(rows_ref, vectors_ref, up_ref, down_ref):
    width, cells = vectors_ref.shape
    count = rows_ref.shape[1]
    lane = lax.broadcasted_iota(jnp.int32, (16, PICK), 0).astype(jnp.int16)
    for direction, picked_ref in enumerate((up_ref, down_ref)):
        for part in range(count // PICK):
            columns = slice(part * PICK, (part + 1) * PICK)
            wanted = rows_ref[direction : direction + 1, columns]
            wanted = jnp.broadcast_to(wanted, (16, PICK)).astype(jnp.int16)

            def step(chunk, total):
                base = pl.multiple_of(chunk * SPAN, SPAN)
                local = wanted - (chunk * SPAN).astype(jnp.int16)
                tile = [
                    jnp.where(local == lane + jnp.int16(16 * row), jnp.bfloat16(1), jnp.bfloat16(0))
                    for row in range(SPAN // 16)
                ]
                return total + jnp.dot(
                    vectors_ref[:, pl.ds(base, SPAN)],
                    jnp.concatenate(tile, axis=0),
                    preferred_element_type=jnp.float32,
                )

            total = lax.fori_loop(0, cells // SPAN, step, jnp.zeros((width, PICK), jnp.float32))
            picked_ref[:, columns] = total.astype(jnp.bfloat16)


def pick(halo_rows, vectors):
    whole = pl.BlockSpec(memory_space=pltpu.VMEM)
    width, cells = vectors.shape
    count = halo_rows.shape[1]
    picked = jax.ShapeDtypeStruct((width, count), jnp.bfloat16)
    return pl.pallas_call(
        pick_kernel,
        out_shape=(picked, picked),
        in_specs=[whole, whole],
        out_specs=(whole, whole),
        cost_estimate=pl.CostEstimate(
            flops=4 * width * cells * count, bytes_accessed=2 * width * cells, transcendentals=0
        ),
        compiler_params=pltpu.CompilerParams(vmem_limit_bytes=VMEM_LIMIT),
    )(halo_rows, vectors)


def ranks(pins):
    rows = [jnp.zeros_like(pins[:1])]
    for slot in range(1, pins.shape[0]):
        same = (pins[:slot] == pins[slot : slot + 1]).astype(jnp.int32)
        rows.append(jnp.sum(same, axis=0, keepdims=True))
    return jnp.concatenate(rows, axis=0)


def spread_pins(stride, turn, pins, place_tile, value_tile):
    slots, block = pins.shape
    field = jnp.zeros(pins.shape, jnp.int32)
    for index in range(1, FIELDS):
        field = field + (pins >= index * stride).astype(jnp.int32)
    rank = ranks(pins)
    mine = (rank >= 3 * turn) & (rank < 3 * turn + 3)
    place = jnp.where(mine, pins - field * stride, -1)
    value = lax.shift_left(jnp.ones_like(field), 2 * field)
    for slot in range(slots):
        place_tile[slot] = jnp.broadcast_to(place[slot : slot + 1, :], (16, block)).astype(jnp.int16)
        value_tile[slot] = jnp.broadcast_to(value[slot : slot + 1, :], (16, block)).astype(jnp.int16)


def build_words(chunk, extent, place_tile, value_tile):
    slots, sublanes, block = place_tile.shape
    lane = lax.broadcasted_iota(jnp.int32, (sublanes, block), 0).astype(jnp.int16)
    local = [place_tile[slot] - (chunk * extent).astype(jnp.int16) for slot in range(slots)]
    rows = []
    for row in range(extent // sublanes):
        here = lane + jnp.int16(sublanes * row)
        word = jnp.zeros((sublanes, block), jnp.int16)
        for slot in range(slots):
            word = word + jnp.where(local[slot] == here, value_tile[slot], jnp.int16(0))
        rows.append(word)
    return jnp.concatenate(rows, axis=0)


def unpack(words, field):
    return (lax.shift_right_logical(words, jnp.int16(2 * field)) & jnp.int16(3)).astype(jnp.bfloat16)


def words_kernel(pins_ref, words_ref, place_tile, value_tile):
    stride = words_ref.shape[0]
    extent = stride // 2
    spread_pins(stride, 0, pins_ref[...], place_tile, value_tile)

    def step(chunk, carry):
        words_ref[pl.ds(pl.multiple_of(chunk * extent, extent), extent), :] = build_words(
            chunk, extent, place_tile, value_tile
        )
        return carry

    lax.fori_loop(0, stride // extent, step, 0)


def count_words(pins, total):
    slots, nets = pins.shape
    stride = total // FIELDS
    return pl.pallas_call(
        words_kernel,
        grid=(nets // BLOCK,),
        out_shape=jax.ShapeDtypeStruct((stride, nets), jnp.int16),
        in_specs=[pl.BlockSpec((slots, BLOCK), lambda step: (0, step))],
        out_specs=pl.BlockSpec((stride, BLOCK), lambda step: (0, step)),
        scratch_shapes=[pltpu.VMEM((slots, 16, BLOCK), jnp.int16)] * 2,
        cost_estimate=pl.CostEstimate(
            flops=24 * stride * nets, bytes_accessed=2 * stride * nets, transcendentals=0
        ),
        compiler_params=pltpu.CompilerParams(vmem_limit_bytes=VMEM_LIMIT),
    )(pins)


def image_kernel(
    words_ref, pins_ref, vectors_ref, prev_ref, next_ref, anchors_ref,
    image_ref, gram_ref,
    extended, contrib, inc_even, inc_odd, t_even, t_odd, sums, place_tile, value_tile,
):
    width, cells = vectors_ref.shape
    bound = prev_ref.shape[1]
    stride = words_ref.shape[0]
    incs = (inc_even, inc_odd)
    scaled = (t_even, t_odd)
    turn = pl.program_id(0)

    def finish(half):
        pins = pins_ref[:, half * BLOCK : (half + 1) * BLOCK]
        size = jnp.sum((pins >= 0).astype(jnp.float32), axis=0, keepdims=True)
        weight = 1.0 / (size - 1.0)
        target = scaled[half]
        target[:width, :] = (sums[...] * weight).astype(jnp.bfloat16)
        degree = weight * size
        first = degree.astype(jnp.bfloat16).astype(jnp.float32)
        second = (degree - first).astype(jnp.bfloat16).astype(jnp.float32)
        third = degree - first - second
        row = lax.broadcasted_iota(jnp.int32, (16, BLOCK), 0)
        parts = jnp.where(row == 0, first, jnp.where(row == 1, second, jnp.where(row == 2, third, 0.0)))
        target[width:, :] = parts.astype(jnp.bfloat16)

    def step(half, gather, spread, owned, chunk):
        base = chunk * CHUNK
        if gather:
            words = words_ref[pl.ds(base, CHUNK), half * BLOCK : (half + 1) * BLOCK]
            fresh = jnp.zeros(sums.shape, jnp.float32)
        for field in range(FIELDS):
            place = field * stride + base
            if spread is not None and field < owned:
                contrib[:, pl.ds(place, CHUNK)] += lax.dot_general(
                    scaled[spread][...],
                    incs[spread][pl.ds(place, CHUNK), :],
                    (((1,), (1,)), ((), ())),
                    preferred_element_type=jnp.float32,
                )
            if gather:
                tile = unpack(words, field)
                if field < owned:
                    incs[half][pl.ds(place, CHUNK), :] = tile
                fresh = fresh + jnp.dot(
                    extended[:, pl.ds(place, CHUNK)], tile, preferred_element_type=jnp.float32
                )
        if gather:
            sums[...] += fresh

    def repeats(half, owned, chunk):
        base = pl.multiple_of(chunk * CHUNK, CHUNK)
        words = build_words(chunk, CHUNK, place_tile, value_tile)
        for field in range(FIELDS):
            place = pl.multiple_of(field * stride + base, CHUNK)
            tile = unpack(words, field)
            if field < owned:
                incs[half][pl.ds(place, CHUNK), :] += tile
            sums[...] += jnp.dot(extended[:, pl.ds(place, CHUNK)], tile, preferred_element_type=jnp.float32)

    many = -(-cells // stride)
    edge = (cells - (many - 1) * stride) // CHUNK

    def over_chunks(work):
        def low(chunk, carry):
            work(many, chunk)
            return carry

        def high(chunk, carry):
            work(many - 1, chunk)
            return carry

        lax.fori_loop(0, edge, low, 0)
        lax.fori_loop(edge, stride // CHUNK, high, 0)

    def sweep(half, gather, spread):
        if gather:
            sums[...] = jnp.zeros_like(sums)
        for chunk in range(stride // CHUNK):
            step(half, gather, spread, many if chunk < edge else many - 1, chunk)
        if gather:
            pins = pins_ref[:, half * BLOCK : (half + 1) * BLOCK]
            most = jnp.max(jnp.where(pins >= 0, ranks(pins), 0))

            @pl.when(most >= 3)
            def _():
                def again(later, carry):
                    spread_pins(stride, later, pins, place_tile, value_tile)
                    over_chunks(functools.partial(repeats, half))
                    return carry

                lax.fori_loop(1, 3, again, 0)

            finish(half)

    @pl.when(turn == 0)
    def _():
        extended[:, :cells] = vectors_ref[...]
        extended[:, cells : cells + bound] = prev_ref[...]
        extended[:, cells + bound :] = next_ref[...]
        contrib[...] = jnp.zeros_like(contrib)
        sweep(0, True, None)

    @pl.when(turn > 0)
    def _():
        sweep(0, True, 1)

    sweep(1, True, 0)

    @pl.when(turn == pl.num_programs(0) - 1)
    def _():
        sweep(1, False, 1)
        degree = (
            contrib[width : width + 1, :] + contrib[width + 1 : width + 2, :] + contrib[width + 2 : width + 3, :]
        )
        image = (degree + anchors_ref[...]) * vectors_ref[...].astype(jnp.float32) - contrib[:width, :]
        image_ref[...] = image
        gram = lax.dot_general(
            image, image, (((1,), (1,)), ((), ())), precision=HIGHEST, preferred_element_type=jnp.float32
        )
        fold = width // 2
        packed = jnp.concatenate([gram[:fold], gram[fold:]], axis=1)
        for copy in range(gram_ref.shape[0]):
            gram_ref[copy] = packed


def image_and_gram(words, pins, vectors, from_prev, from_next, anchors, copies):
    width, cells = vectors.shape
    slots, nets = pins.shape
    stride = words.shape[0]
    whole = pl.BlockSpec(memory_space=pltpu.VMEM)
    return pl.pallas_call(
        image_kernel,
        grid=(nets // (2 * BLOCK),),
        out_shape=(
            jax.ShapeDtypeStruct((width, cells), jnp.float32),
            jax.ShapeDtypeStruct((copies, width // 2, 2 * width), jnp.float32),
        ),
        in_specs=[
            pl.BlockSpec((stride, 2 * BLOCK), lambda step: (0, step)),
            pl.BlockSpec((slots, 2 * BLOCK), lambda step: (0, step)),
        ]
        + [whole] * 4,
        out_specs=(whole, whole),
        scratch_shapes=[
            pltpu.VMEM((width, stride * FIELDS), jnp.bfloat16),
            pltpu.VMEM((width + 16, cells), jnp.float32),
            pltpu.VMEM((cells, BLOCK), jnp.bfloat16),
            pltpu.VMEM((cells, BLOCK), jnp.bfloat16),
            pltpu.VMEM((width + 16, BLOCK), jnp.bfloat16),
            pltpu.VMEM((width + 16, BLOCK), jnp.bfloat16),
            pltpu.VMEM((width, BLOCK), jnp.float32),
            pltpu.VMEM((slots, 16, BLOCK), jnp.int16),
            pltpu.VMEM((slots, 16, BLOCK), jnp.int16),
        ],
        compiler_params=pltpu.CompilerParams(vmem_limit_bytes=VMEM_LIMIT),
    )(words, pins, vectors, from_prev, from_next, anchors[None, :])


def summed_gram(copies):
    groups = lax.axis_size("wide")
    pairs = [[2 * chip, 2 * chip + 1] for chip in range(groups // 2)]
    columns = [[2 * chip + core for chip in range(groups // 2)] for core in range(2)]
    plane = jnp.sum(lax.all_to_all(copies, "narrow", 0, 0), axis=0)
    plane = jnp.sum(lax.all_gather(plane, "wide", axis_index_groups=pairs), axis=0)
    half = plane.shape[0] // 2
    start = lax.rem(lax.axis_index("wide"), 2) * half
    share = lax.dynamic_slice_in_dim(plane, start, half, axis=0)
    share = jnp.broadcast_to(share[None], (groups // 2,) + share.shape)
    share = jnp.sum(lax.all_to_all(share, "wide", 0, 0, axis_index_groups=columns), axis=0)
    return lax.all_gather(share, "wide", axis_index_groups=pairs, tiled=True)


def factor_kernel(scale, gram_ref, image_ref, embedding_ref, factor_ref):
    width = gram_ref.shape[1] // 2
    gram = jnp.concatenate([gram_ref[:, :width], gram_ref[:, width:]], axis=0)
    rows = lax.broadcasted_iota(jnp.int32, (width, 2 * width), 0)
    columns = lax.broadcasted_iota(jnp.int32, (width, 2 * width), 1)
    unit = (columns == rows + width).astype(jnp.float32)
    work = jnp.concatenate([gram, jnp.zeros((width, width), jnp.float32)], axis=1) + unit
    pivots = []
    for index in range(0, width, GROUP):
        base = index // 8 * 8
        part = work[base:]
        below = rows[base:]
        first = index - base
        spread = [jnp.broadcast_to(part[:, index + item : index + item + 1], part.shape) for item in range(GROUP)]
        lines = [part[first + item : first + item + 1] for item in range(GROUP)]
        for item in range(GROUP):
            here = first + item
            pivot = spread[item][here : here + 1]
            pivots.append(pivot)
            inverse = 1.0 / pivot
            column = jnp.where(below > index + item, spread[item], 0.0)
            line = lines[item] * inverse
            for other in range(item + 1, GROUP):
                ratio = spread[other][here : here + 1] * inverse
                spread[other] = spread[other] - column * ratio
                lines[other] = lines[other] - column[first + other : first + other + 1] * line
            part = part - column * line
        work = jnp.concatenate([work[:base], part], axis=0) if base else part
    work = work / jnp.sqrt(jnp.concatenate(pivots, axis=0))
    upper = columns[:, :width] >= rows[:, :width]
    factor_ref[...] = jnp.where(upper, work[:, :width], 0.0) / scale
    embedding_ref[...] = jnp.dot(
        work[:, width:] * scale, image_ref[...], precision=HIGHEST, preferred_element_type=jnp.float32
    )


def factor_and_embed(gram, image, scale):
    whole = pl.BlockSpec(memory_space=pltpu.VMEM)
    return pl.pallas_call(
        functools.partial(factor_kernel, scale),
        out_shape=(
            jax.ShapeDtypeStruct(image.shape, jnp.float32),
            jax.ShapeDtypeStruct((image.shape[0],) * 2, jnp.float32),
        ),
        in_specs=[whole, whole],
        out_specs=(whole, whole),
        compiler_params=pltpu.CompilerParams(vmem_limit_bytes=VMEM_LIMIT),
    )(gram, image)


def body(vectors, anchors, pins, halo_rows):
    cells = vectors.shape[1]
    total = cells + halo_rows.size
    up, down = pick(halo_rows, vectors)
    from_prev = shifted(up, 1)
    from_next = shifted(down, -1)
    words = count_words(pins, total)
    copies = lax.axis_size("narrow")
    image, gram = image_and_gram(words, pins, vectors, from_prev, from_next, anchors, copies)
    gram = summed_gram(gram)
    scale = float(cells * lax.axis_size(BOTH)) ** 0.5
    return factor_and_embed(gram, image, scale)


def solution(mesh):
    in_specs = (P(None, BOTH), P(BOTH), P(None, BOTH), P(None, BOTH))
    out_specs = (P(None, BOTH), P())
    return jax.shard_map(body, mesh=mesh, in_specs=in_specs, out_specs=out_specs, check_vma=False)
```

```python
import functools

import jax
import jax.numpy as jnp
from jax import lax
from jax.experimental import pallas as pl
from jax.experimental.pallas import tpu as pltpu
from jax.sharding import PartitionSpec as P

BOTH = ("wide", "narrow")
HIGHEST = lax.Precision.HIGHEST
BLOCK = 512
CHUNK = 256
FIELDS = 8
PICK = 512
SPAN = 4096
GROUP = 8
WIDE = 1024
VMEM_LIMIT = 60 << 20


def shifted(value, steps):
    count = lax.axis_size(BOTH)
    pairs = [(source, (source + steps) % count) for source in range(count)]
    return lax.ppermute(value, BOTH, pairs)


def pick_kernel(rows_ref, vectors_ref, up_ref, down_ref):
    width, cells = vectors_ref.shape
    count = rows_ref.shape[1]
    lane = lax.broadcasted_iota(jnp.int32, (16, PICK), 0).astype(jnp.int16)
    for direction, picked_ref in enumerate((up_ref, down_ref)):
        for part in range(count // PICK):
            columns = slice(part * PICK, (part + 1) * PICK)
            wanted = rows_ref[direction : direction + 1, columns]
            wanted = jnp.broadcast_to(wanted, (16, PICK)).astype(jnp.int16)

            def step(chunk, total):
                base = pl.multiple_of(chunk * SPAN, SPAN)
                local = wanted - (chunk * SPAN).astype(jnp.int16)
                tile = [
                    jnp.where(local == lane + jnp.int16(16 * row), jnp.bfloat16(1), jnp.bfloat16(0))
                    for row in range(SPAN // 16)
                ]
                return total + jnp.dot(
                    vectors_ref[:, pl.ds(base, SPAN)],
                    jnp.concatenate(tile, axis=0),
                    preferred_element_type=jnp.float32,
                )

            total = lax.fori_loop(0, cells // SPAN, step, jnp.zeros((width, PICK), jnp.float32))
            picked_ref[:, columns] = total.astype(jnp.bfloat16)


def pick(halo_rows, vectors):
    whole = pl.BlockSpec(memory_space=pltpu.VMEM)
    width, cells = vectors.shape
    count = halo_rows.shape[1]
    picked = jax.ShapeDtypeStruct((width, count), jnp.bfloat16)
    return pl.pallas_call(
        pick_kernel,
        out_shape=(picked, picked),
        in_specs=[whole, whole],
        out_specs=(whole, whole),
        cost_estimate=pl.CostEstimate(
            flops=4 * width * cells * count, bytes_accessed=2 * width * cells, transcendentals=0
        ),
        compiler_params=pltpu.CompilerParams(vmem_limit_bytes=VMEM_LIMIT),
    )(halo_rows, vectors)


def ranks(pins):
    rows = [jnp.zeros_like(pins[:1])]
    for slot in range(1, pins.shape[0]):
        same = (pins[:slot] == pins[slot : slot + 1]).astype(jnp.int32)
        rows.append(jnp.sum(same, axis=0, keepdims=True))
    return jnp.concatenate(rows, axis=0)


def spread_pins(stride, turn, pins, place_tile, value_tile):
    slots, block = pins.shape
    field = jnp.zeros(pins.shape, jnp.int32)
    for index in range(1, FIELDS):
        field = field + (pins >= index * stride).astype(jnp.int32)
    rank = ranks(pins)
    mine = (rank >= 3 * turn) & (rank < 3 * turn + 3)
    place = jnp.where(mine, pins - field * stride, -1)
    value = lax.shift_left(jnp.ones_like(field), 2 * field)
    for slot in range(slots):
        place_tile[slot] = jnp.broadcast_to(place[slot : slot + 1, :], (16, block)).astype(jnp.int16)
        value_tile[slot] = jnp.broadcast_to(value[slot : slot + 1, :], (16, block)).astype(jnp.int16)


def build_words(chunk, extent, place_tile, value_tile):
    slots, sublanes, block = place_tile.shape
    lane = lax.broadcasted_iota(jnp.int32, (sublanes, block), 0).astype(jnp.int16)
    local = [place_tile[slot] - (chunk * extent).astype(jnp.int16) for slot in range(slots)]
    rows = []
    for row in range(extent // sublanes):
        here = lane + jnp.int16(sublanes * row)
        word = jnp.zeros((sublanes, block), jnp.int16)
        for slot in range(slots):
            word = word + jnp.where(local[slot] == here, value_tile[slot], jnp.int16(0))
        rows.append(word)
    return jnp.concatenate(rows, axis=0)


def unpack(words, field):
    return (lax.shift_right_logical(words, jnp.int16(2 * field)) & jnp.int16(3)).astype(jnp.bfloat16)


def words_kernel(pins_ref, words_ref, place_tile, value_tile):
    stride = words_ref.shape[0]
    extent = stride // 2
    spread_pins(stride, 0, pins_ref[...], place_tile, value_tile)

    def step(chunk, carry):
        words_ref[pl.ds(pl.multiple_of(chunk * extent, extent), extent), :] = build_words(
            chunk, extent, place_tile, value_tile
        )
        return carry

    lax.fori_loop(0, stride // extent, step, 0)


def count_words(pins, total):
    slots, nets = pins.shape
    stride = total // FIELDS
    return pl.pallas_call(
        words_kernel,
        grid=(nets // WIDE,),
        out_shape=jax.ShapeDtypeStruct((stride, nets), jnp.int16),
        in_specs=[pl.BlockSpec((slots, WIDE), lambda step: (0, step))],
        out_specs=pl.BlockSpec((stride, WIDE), lambda step: (0, step)),
        scratch_shapes=[pltpu.VMEM((slots, 16, WIDE), jnp.int16)] * 2,
        cost_estimate=pl.CostEstimate(
            flops=24 * stride * nets, bytes_accessed=2 * stride * nets, transcendentals=0
        ),
        compiler_params=pltpu.CompilerParams(vmem_limit_bytes=VMEM_LIMIT),
    )(pins)


def image_kernel(
    words_ref, pins_ref, vectors_ref, prev_ref, next_ref, anchors_ref,
    image_ref, gram_ref,
    extended, contrib, inc_even, inc_odd, t_even, t_odd, sums, place_tile, value_tile,
):
    width, cells = vectors_ref.shape
    bound = prev_ref.shape[1]
    stride = words_ref.shape[0]
    incs = (inc_even, inc_odd)
    scaled = (t_even, t_odd)
    turn = pl.program_id(0)

    def finish(half):
        pins = pins_ref[:, half * BLOCK : (half + 1) * BLOCK]
        size = jnp.sum((pins >= 0).astype(jnp.float32), axis=0, keepdims=True)
        weight = 1.0 / (size - 1.0)
        target = scaled[half]
        target[:width, :] = (sums[...] * weight).astype(jnp.bfloat16)
        degree = weight * size
        first = degree.astype(jnp.bfloat16).astype(jnp.float32)
        second = (degree - first).astype(jnp.bfloat16).astype(jnp.float32)
        third = degree - first - second
        row = lax.broadcasted_iota(jnp.int32, (16, BLOCK), 0)
        parts = jnp.where(row == 0, first, jnp.where(row == 1, second, jnp.where(row == 2, third, 0.0)))
        target[width:, :] = parts.astype(jnp.bfloat16)

    def step(half, gather, spread, owned, chunk):
        base = chunk * CHUNK
        if gather:
            words = words_ref[pl.ds(base, CHUNK), half * BLOCK : (half + 1) * BLOCK]
        for field in range(FIELDS):
            place = field * stride + base
            if spread is not None and field < owned:
                contrib[:, pl.ds(place, CHUNK)] += lax.dot_general(
                    scaled[spread][...],
                    incs[spread][pl.ds(place, CHUNK), :],
                    (((1,), (1,)), ((), ())),
                    preferred_element_type=jnp.float32,
                )
            if gather:
                tile = unpack(words, field)
                if field < owned:
                    incs[half][pl.ds(place, CHUNK), :] = tile
                sums[...] += jnp.dot(extended[:, pl.ds(place, CHUNK)], tile, preferred_element_type=jnp.float32)

    def repeats(half, owned, chunk):
        base = pl.multiple_of(chunk * CHUNK, CHUNK)
        words = build_words(chunk, CHUNK, place_tile, value_tile)
        for field in range(FIELDS):
            place = pl.multiple_of(field * stride + base, CHUNK)
            tile = unpack(words, field)
            if field < owned:
                incs[half][pl.ds(place, CHUNK), :] += tile
            sums[...] += jnp.dot(extended[:, pl.ds(place, CHUNK)], tile, preferred_element_type=jnp.float32)

    many = -(-cells // stride)
    edge = (cells - (many - 1) * stride) // CHUNK

    def over_chunks(work):
        def low(chunk, carry):
            work(many, chunk)
            return carry

        def high(chunk, carry):
            work(many - 1, chunk)
            return carry

        lax.fori_loop(0, edge, low, 0)
        lax.fori_loop(edge, stride // CHUNK, high, 0)

    def sweep(half, gather, spread):
        if gather:
            sums[...] = jnp.zeros_like(sums)
        for chunk in range(stride // CHUNK):
            step(half, gather, spread, many if chunk < edge else many - 1, chunk)
        if gather:
            pins = pins_ref[:, half * BLOCK : (half + 1) * BLOCK]
            most = jnp.max(jnp.where(pins >= 0, ranks(pins), 0))

            @pl.when(most >= 3)
            def _():
                def again(later, carry):
                    spread_pins(stride, later, pins, place_tile, value_tile)
                    over_chunks(functools.partial(repeats, half))
                    return carry

                lax.fori_loop(1, 3, again, 0)

            finish(half)

    @pl.when(turn == 0)
    def _():
        extended[:, :cells] = vectors_ref[...]
        extended[:, cells : cells + bound] = prev_ref[...]
        extended[:, cells + bound :] = next_ref[...]
        contrib[...] = jnp.zeros_like(contrib)
        sweep(0, True, None)

    @pl.when(turn > 0)
    def _():
        sweep(0, True, 1)

    sweep(1, True, 0)

    @pl.when(turn == pl.num_programs(0) - 1)
    def _():
        sweep(1, False, 1)
        degree = (
            contrib[width : width + 1, :] + contrib[width + 1 : width + 2, :] + contrib[width + 2 : width + 3, :]
        )
        image = (degree + anchors_ref[...]) * vectors_ref[...].astype(jnp.float32) - contrib[:width, :]
        image_ref[...] = image
        gram = lax.dot_general(
            image, image, (((1,), (1,)), ((), ())), precision=HIGHEST, preferred_element_type=jnp.float32
        )
        fold = width // 2
        packed = jnp.concatenate([gram[:fold], gram[fold:]], axis=1)
        for copy in range(gram_ref.shape[0]):
            gram_ref[copy] = packed


def image_and_gram(words, pins, vectors, from_prev, from_next, anchors, copies):
    width, cells = vectors.shape
    slots, nets = pins.shape
    stride = words.shape[0]
    whole = pl.BlockSpec(memory_space=pltpu.VMEM)
    return pl.pallas_call(
        image_kernel,
        grid=(nets // (2 * BLOCK),),
        out_shape=(
            jax.ShapeDtypeStruct((width, cells), jnp.float32),
            jax.ShapeDtypeStruct((copies, width // 2, 2 * width), jnp.float32),
        ),
        in_specs=[
            pl.BlockSpec((stride, 2 * BLOCK), lambda step: (0, step)),
            pl.BlockSpec((slots, 2 * BLOCK), lambda step: (0, step)),
        ]
        + [whole] * 4,
        out_specs=(whole, whole),
        scratch_shapes=[
            pltpu.VMEM((width, stride * FIELDS), jnp.bfloat16),
            pltpu.VMEM((width + 16, cells), jnp.float32),
            pltpu.VMEM((cells, BLOCK), jnp.bfloat16),
            pltpu.VMEM((cells, BLOCK), jnp.bfloat16),
            pltpu.VMEM((width + 16, BLOCK), jnp.bfloat16),
            pltpu.VMEM((width + 16, BLOCK), jnp.bfloat16),
            pltpu.VMEM((width, BLOCK), jnp.float32),
            pltpu.VMEM((slots, 16, BLOCK), jnp.int16),
            pltpu.VMEM((slots, 16, BLOCK), jnp.int16),
        ],
        compiler_params=pltpu.CompilerParams(vmem_limit_bytes=VMEM_LIMIT),
    )(words, pins, vectors, from_prev, from_next, anchors[None, :])


def summed_gram(copies):
    groups = lax.axis_size("wide")
    pairs = [[2 * chip, 2 * chip + 1] for chip in range(groups // 2)]
    columns = [[2 * chip + core for chip in range(groups // 2)] for core in range(2)]
    plane = jnp.sum(lax.all_to_all(copies, "narrow", 0, 0), axis=0)
    plane = jnp.sum(lax.all_gather(plane, "wide", axis_index_groups=pairs), axis=0)
    half = plane.shape[0] // 2
    start = lax.rem(lax.axis_index("wide"), 2) * half
    share = lax.dynamic_slice_in_dim(plane, start, half, axis=0)
    share = jnp.broadcast_to(share[None], (groups // 2,) + share.shape)
    share = jnp.sum(lax.all_to_all(share, "wide", 0, 0, axis_index_groups=columns), axis=0)
    return lax.all_gather(share, "wide", axis_index_groups=pairs, tiled=True)


def factor_kernel(scale, gram_ref, image_ref, embedding_ref, factor_ref):
    width = gram_ref.shape[1] // 2
    gram = jnp.concatenate([gram_ref[:, :width], gram_ref[:, width:]], axis=0)
    rows = lax.broadcasted_iota(jnp.int32, (width, 2 * width), 0)
    columns = lax.broadcasted_iota(jnp.int32, (width, 2 * width), 1)
    unit = (columns == rows + width).astype(jnp.float32)
    work = jnp.concatenate([gram, jnp.zeros((width, width), jnp.float32)], axis=1) + unit
    pivots = []
    for index in range(0, width, GROUP):
        base = index // 8 * 8
        part = work[base:]
        below = rows[base:]
        first = index - base
        spread = [jnp.broadcast_to(part[:, index + item : index + item + 1], part.shape) for item in range(GROUP)]
        lines = [part[first + item : first + item + 1] for item in range(GROUP)]
        for item in range(GROUP):
            here = first + item
            pivot = spread[item][here : here + 1]
            pivots.append(pivot)
            inverse = 1.0 / pivot
            column = jnp.where(below > index + item, spread[item], 0.0)
            line = lines[item] * inverse
            for other in range(item + 1, GROUP):
                ratio = spread[other][here : here + 1] * inverse
                spread[other] = spread[other] - column * ratio
                lines[other] = lines[other] - column[first + other : first + other + 1] * line
            part = part - column * line
        work = jnp.concatenate([work[:base], part], axis=0) if base else part
    work = work / jnp.sqrt(jnp.concatenate(pivots, axis=0))
    upper = columns[:, :width] >= rows[:, :width]
    factor_ref[...] = jnp.where(upper, work[:, :width], 0.0) / scale
    embedding_ref[...] = jnp.dot(
        work[:, width:] * scale, image_ref[...], precision=HIGHEST, preferred_element_type=jnp.float32
    )


def factor_and_embed(gram, image, scale):
    whole = pl.BlockSpec(memory_space=pltpu.VMEM)
    return pl.pallas_call(
        functools.partial(factor_kernel, scale),
        out_shape=(
            jax.ShapeDtypeStruct(image.shape, jnp.float32),
            jax.ShapeDtypeStruct((image.shape[0],) * 2, jnp.float32),
        ),
        in_specs=[whole, whole],
        out_specs=(whole, whole),
        compiler_params=pltpu.CompilerParams(vmem_limit_bytes=VMEM_LIMIT),
    )(gram, image)


def body(vectors, anchors, pins, halo_rows):
    cells = vectors.shape[1]
    total = cells + halo_rows.size
    up, down = pick(halo_rows, vectors)
    from_prev = shifted(up, 1)
    from_next = shifted(down, -1)
    words = count_words(pins, total)
    copies = lax.axis_size("narrow")
    image, gram = image_and_gram(words, pins, vectors, from_prev, from_next, anchors, copies)
    gram = summed_gram(gram)
    scale = float(cells * lax.axis_size(BOTH)) ** 0.5
    return factor_and_embed(gram, image, scale)


def solution(mesh):
    in_specs = (P(None, BOTH), P(BOTH), P(None, BOTH), P(None, BOTH))
    out_specs = (P(None, BOTH), P())
    return jax.shard_map(body, mesh=mesh, in_specs=in_specs, out_specs=out_specs, check_vma=False)
```
